32 devices in a mesh: parts: 2 (over y), freq: 4 (over z), pan: 2 (over x), rep: 2 (over core).
Axes of the slice: x: 2, y: 2, z: 4, core: 2. Of those that a mesh axis runs over, the one named last changes fastest.
Arguments:
- traces: bfloat16 [2048, 4096], P(('parts', 'freq', 'pan', 'rep')), parts along dimension 0, may hold values from -6 to 6
- data: bfloat16 [8, 2, 2048, 2048], P(('parts', 'freq'), None, ('pan', 'rep')), parts along dimension 0, may hold values from -1.5 to 1.5
- trace_shot: int32 [2048], P('parts'), parts along dimension 0, may hold values from 0 to 2047, as said below
- trace_recv: int32 [2048], P('parts'), parts along dimension 0, may hold values from 0 to 2047
- aper_panel: int32 [8, 4], P('parts'), parts along dimension 0, may hold values from 0 to 15
- aper_order: int32 [8, 4], P('parts'), parts along dimension 0, may hold values from 0 to 3, each once within a row
- aper_count: int32 [8], P('parts'), parts along dimension 0, may hold values from 1 to 4, as said below
Outputs:
- multiples: bfloat16 [8, 2, 2048, 2048], P(('parts', 'freq'), None, ('pan', 'rep')), parts along dimension 0
- primaries: float32 [2048, 2, 4], P(('parts', 'freq', 'pan', 'rep')), parts along dimension 0
The draws below stay inside these ranges and needn't reach their ends.
There are 2 independent parts, one for each index of `parts`. The reference program is written for one: setup_inputs(seed, part) draws one part's arguments, and reference() takes and returns one part's arrays. A program takes and returns all parts, laid end to end along the dimension named above; each array names one. Nothing has to cross between parts.
Inputs may be any that keep to these rules, and one draw needn't show every extreme that they name: `trace_shot`: among the 64 traces of each aligned block (one device's traces), at most 32 have shots of one group of 512 shots, and some group has exactly 32. `aper_count`: some group's aperture takes all 4 groups.
All inputs are finite; a program needn't handle non-finite values.
Results may differ from the reference program's by a relative error of at most 0.0034.
Values may be sent and summed in bfloat16 or wider, within the bound.
A program may use at most 192 MiB of HBM per device.

```python
import math
import jax
import jax.numpy as jnp
from jax import lax

NS = 2048
NT = 4096
KB = 32
FBIN0 = 64
FSTEP = 3
TR_DEV = 64
READERS = 4
SB = 512
PPD = 16
CAPT = 32
NF = 4
TRACES = 1024


def draw_trace_shot(key, part):
    key = jax.random.fold_in(key, 11)
    blocks = TRACES // TR_DEV

    def per_block(block_key):
        first, second, third, fourth = jax.random.split(block_key, 4)
        forced = jax.random.randint(first, (), 0, READERS)
        others = jax.random.permutation(second, (READERS - 1) * CAPT) // CAPT
        others = (others + (others >= forced).astype(jnp.int32)).astype(jnp.int32)
        listed = jnp.concatenate([jnp.full((CAPT,), forced, jnp.int32), others[:TR_DEV - CAPT]])
        listed = jax.random.permutation(third, listed)
        offset = jax.random.randint(fourth, (TR_DEV,), 0, SB)
        return (listed * SB + offset).astype(jnp.int32)
    return jax.vmap(per_block)(jax.random.split(key, blocks)).reshape(-1).astype(jnp.int32)


def draw_aper_count(key, part):
    key = jax.random.fold_in(key, 23)
    first, second = jax.random.split(key)
    counts = jax.random.randint(first, (READERS,), 1, READERS + 1)
    widest = jax.random.randint(second, (), 0, READERS)
    return counts.at[widest].set(READERS).astype(jnp.int32)


def set_ends(entries, own_key, low, top_value):
    longest = entries.shape.index(max(entries.shape))
    spots = []
    for shift in (0, 1):
        where = [jax.random.randint(jax.random.fold_in(own_key, axis), (), 0, length) for axis, length in enumerate(entries.shape)]
        where[longest] = (where[longest] + shift) % entries.shape[longest]
        spots.append(tuple(where))
    return entries.at[spots[0]].set(low).at[spots[1]].set(top_value)


def block_scale(own_key, dims, cuts, smallest, largest):
    loudness = 1.0
    for dim, parts in cuts:
        steps = jax.random.uniform(jax.random.fold_in(jax.random.fold_in(own_key, 6), dim), (parts,), jnp.float32, smallest / len(cuts), largest / len(cuts))
        loudness = loudness * jnp.repeat(jnp.exp(steps), dims[dim] // parts).reshape((-1,) + (1,) * (len(dims) - 1 - dim))
    return loudness


def centred(stream_key, dims, scale, limit, cuts=(), held_as=jnp.bfloat16):
    drawn = jax.random.normal(stream_key, dims, jnp.float32) * scale
    if len(cuts) > 0:
        drawn = block_scale(stream_key, dims, cuts, -0.22, 0.18) * drawn
    return jnp.clip(drawn, min=-limit, max=limit).astype(held_as)


def setup_inputs(seed: int = 0, part: int = 0) -> dict:
    seeds = jax.random.split(jax.random.key(seed), 8)
    part_keys = jax.random.split(jax.random.fold_in(seeds[7], part), 8)
    return {
        "traces": centred(part_keys[0], (TRACES, NT), 1.0, 6.0, ((0, 16),)),
        "data": centred(part_keys[1], (NF, 2, NS, NS), 0.25, 1.5, ((0, 4), (2, 4))),
        "trace_shot": draw_trace_shot(jax.random.fold_in(jax.random.fold_in(seeds[7], part), 71), part),
        "trace_recv": set_ends(jax.random.randint(part_keys[3], (TRACES,), 0, NS), jax.random.fold_in(part_keys[3], 1), 0, NS - 1).astype(jnp.int32),
        "aper_panel": set_ends(jax.random.randint(part_keys[4], (READERS, READERS), 0, PPD), jax.random.fold_in(part_keys[4], 1), 0, PPD - 1).astype(jnp.int32),
        "aper_order": jax.vmap(lambda own: jax.random.permutation(own, READERS))(jax.random.split(part_keys[5], READERS)).reshape((READERS, READERS)).astype(jnp.int32),
        "aper_count": draw_aper_count(jax.random.fold_in(jax.random.fold_in(seeds[7], part), 71), part),
    }


def spectral_table(samples, count, first, stride):
    times = jnp.arange(samples, dtype=jnp.int32)
    bins = first + stride * jnp.arange(count, dtype=jnp.int32)
    phase = times[:, None] * bins[None, :] % samples
    angle = phase.astype(jnp.float32) * (2.0 * math.pi / samples)
    factor = 1.0 / math.sqrt(samples)
    return jnp.concatenate([jnp.cos(angle) * factor, -jnp.sin(angle) * factor], axis=1).astype(jnp.bfloat16)

def membership(order, counts):
    width = order.shape[0]
    position = jnp.arange(width, dtype=jnp.int32)
    within = position[None, :] < counts[:, None]
    hits = (order[:, :, None] == position[None, None, :]) & within[:, :, None]
    return jnp.any(hits, axis=1).astype(jnp.float32)

def reference(traces, data, trace_shot, trace_recv, aper_panel, aper_order, aper_count):
    table = spectral_table(NT, NF, FBIN0, FSTEP)
    spectrum = jnp.dot(traces, table, preferred_element_type=jnp.float32).astype(jnp.bfloat16)
    spectrum = spectrum.reshape(TRACES, 2, NF)
    used = membership(aper_order, aper_count)
    owners = jnp.arange(READERS, dtype=jnp.int32)
    columns = ((owners[None, :] * PPD + aper_panel)[:, :, None] * KB + jnp.arange(KB, dtype=jnp.int32)[None, None, :]).reshape(READERS, READERS * KB)
    live_cols = jnp.repeat(used, KB, axis=1)

    def per_frequency(slab):
        widened = slab.astype(jnp.float32)

        def per_reader(packed):
            group, picks, weights = packed
            strip_rows = lax.dynamic_slice_in_dim(widened, group * SB, SB, 1)
            left_block = jnp.take(strip_rows, picks, axis=2) * weights[None, None, :]
            panel_rows = jnp.take(widened, picks, axis=1)
            real_part = jnp.dot(left_block[0], panel_rows[0], precision=lax.Precision.HIGHEST) - jnp.dot(left_block[1], panel_rows[1], precision=lax.Precision.HIGHEST)
            imag_part = jnp.dot(left_block[0], panel_rows[1], precision=lax.Precision.HIGHEST) + jnp.dot(left_block[1], panel_rows[0], precision=lax.Precision.HIGHEST)
            return jnp.stack([real_part, imag_part], axis=0)
        stacked = lax.map(per_reader, (owners, columns, live_cols))
        return jnp.transpose(stacked, (1, 0, 2, 3)).reshape(2, NS, NS).astype(jnp.bfloat16)
    multiples = lax.map(per_frequency, data)
    picked = jnp.transpose(multiples[:, :, trace_shot, trace_recv], (2, 1, 0))
    primaries = spectrum.astype(jnp.float32) - picked.astype(jnp.float32)
    return (multiples, primaries)
```

```python
import functools
import math

import jax
import jax.numpy as jnp
import numpy as np
from jax import lax
from jax.experimental import pallas as pl
from jax.experimental.pallas import tpu as pltpu
from jax.sharding import PartitionSpec as P

KB = 32
FBIN0 = 64
FSTEP = 3
LANES = 128
CHUNKS = 4
BLOCK = 2 * LANES
MESH = pl.DeviceIdType.MESH
BF = jnp.bfloat16
F32 = jnp.float32


def spectral_table(samples, count, first, stride):
    times = np.arange(samples, dtype=np.int32)
    bins = first + stride * np.arange(count, dtype=np.int32)
    phase = bins[:, None] * times[None, :] % samples
    angle = phase.astype(np.float32) * np.float32(2.0 * math.pi / samples)
    factor = np.float32(1.0 / math.sqrt(samples))
    rows = np.concatenate([np.cos(angle) * factor, -np.sin(angle) * factor], axis=0)
    padded = np.zeros((-(-rows.shape[0] // 16) * 16, samples), np.float32)
    padded[: rows.shape[0]] = rows
    return padded.astype(jnp.bfloat16)


def kernel(
    sizes,
    data_hbm, traces_hbm, table_hbm, panel_s, order_s, count_s, shot_v, recv_v,
    out_hbm, prim_v,
    data_v, traces_v, table_v, send, panels, sel, left_a, left_b, left_t, hot, lsel, acc, picks,
    arrived, tidy, stage,
    load_sem, send_sem, recv_sem, pick_send, pick_recv, out_sem,
):
    NF, PAN, REP, SW, NS, TL, GROUP = sizes
    R = PAN * REP
    N = NF * R
    RK = R * KB
    W = NS // CHUNKS
    PB = LANES // TL
    freq, pan, rep = lax.axis_index("freq"), lax.axis_index("pan"), lax.axis_index("rep")
    reader = pan * REP + rep
    me = freq * R + reader

    def place(s):
        r = lax.rem(s, R)
        return {"freq": lax.div(s, R), "pan": lax.div(r, REP), "rep": lax.rem(r, REP)}

    loads = [
        pltpu.make_async_copy(data_hbm.at[0], data_v, load_sem.at[0]),
        pltpu.make_async_copy(traces_hbm, traces_v, load_sem.at[1]),
        pltpu.make_async_copy(table_hbm, table_v, load_sem.at[2]),
    ]
    for copy in loads:
        copy.start()

    barrier = pltpu.get_barrier_semaphore()

    @pl.loop(1, N)
    def _(k):
        pl.semaphore_signal(
            barrier, inc=1, device_id=place(lax.rem(me + k, N)), device_id_type=MESH
        )

    loads[0].wait()
    offsets = [(dp, dr) for dp in range(PAN) for dr in range(REP) if (dp, dr) != (0, 0)]
    offsets = [o for o in offsets if o[0]] + [o for o in offsets if not o[0]]

    for n, (dp, dr) in enumerate(offsets):
        p = panel_s[lax.rem(pan + dp, PAN) * REP + lax.rem(rep + dr, REP), reader]
        for c in range(CHUNKS):
            send[n, c] = data_v[:, p, :, c * W : (c + 1) * W]
    pl.semaphore_wait(barrier, N - 1)

    def panel_copy(n, c, slot):
        dp, dr = offsets[n]
        return pltpu.make_async_remote_copy(
            src_ref=send.at[n, c],
            dst_ref=panels.at[c, :, slot],
            send_sem=send_sem.at[n, c],
            recv_sem=recv_sem.at[n, c],
            device_id={"pan": lax.rem(pan + dp, PAN), "rep": lax.rem(rep + dr, REP)},
            device_id_type=MESH,
        )

    for c in range(CHUNKS):
        for n in range(R - 1):
            panel_copy(n, c, reader).start()
    p = panel_s[reader, reader]
    for c in range(CHUNKS):
        panels[c, :, reader] = data_v[:, p, :, c * W : (c + 1) * W]

    lane = lax.broadcasted_iota(jnp.int32, (1, RK), 1)
    column = jnp.full((1, RK), -1, jnp.int32)
    for q in range(R):
        hit = jnp.int32(0)
        for m in range(R):
            named = (order_s[reader, m] == q).astype(jnp.int32)
            hit = hit + named * (count_s[reader] > m).astype(jnp.int32)
        base = hit * (q * SW + panel_s[reader, q] * KB - q * KB + 2 * NS) - 2 * NS
        column = jnp.where((lane >= q * KB) & (lane < (q + 1) * KB), lane + base, column)

    @pl.loop(0, NS // 256)
    def _(b):
        at = pl.multiple_of(b * 256, 256)
        rows = lax.broadcasted_iota(jnp.int32, (256, RK), 0) + at
        sel[pl.ds(at, 256), :] = jnp.where(rows == column, 1.0, 0.0).astype(BF)

    @pl.loop(0, SW // 128)
    def _(b):
        rows = pl.ds(pl.multiple_of(b * 128, 128), 128)
        strips = pl.ds(b * (128 // KB), 128 // KB)
        real = jnp.dot(
            data_v[0, strips].reshape(128, NS), sel[...], preferred_element_type=F32
        )
        imag = jnp.dot(
            data_v[1, strips].reshape(128, NS), sel[...], preferred_element_type=F32
        )
        left_a[rows, :RK] = real.astype(BF)
        left_a[rows, RK:] = (-imag).astype(BF)
        left_b[rows, :RK] = imag.astype(BF)
        left_b[rows, RK:] = real.astype(BF)

    left_t[...] = left_a[...].T

    loads[1].wait()
    loads[2].wait()
    spectrum = lax.dot_general(
        table_v[...], traces_v[...], (((1,), (1,)), ((), ())), preferred_element_type=F32
    ).astype(BF)

    blocks = GROUP // BLOCK

    def prepare(g):
        @pl.loop(0, blocks)
        def _(b):
            lanes = pl.ds(pl.multiple_of(b * BLOCK, BLOCK), BLOCK)
            row = (g * blocks + b) * 2
            recv = jnp.concatenate([recv_v[pl.ds(row, 1), :], recv_v[pl.ds(row + 1, 1), :]], axis=1)
            shot = jnp.concatenate([shot_v[pl.ds(row, 1), :], shot_v[pl.ds(row + 1, 1), :]], axis=1)
            for c in range(NS // 256):
                rows = lax.broadcasted_iota(jnp.int32, (256, BLOCK), 0) + c * 256
                hot[c * 256 : (c + 1) * 256, lanes] = jnp.where(rows == recv, 1.0, 0.0).astype(BF)
            mine = lax.broadcasted_iota(jnp.int32, (SW, BLOCK), 0) + reader * SW
            mine = jnp.where(mine == shot, 1.0, 0.0).astype(BF)
            lsel[:, lanes] = jnp.dot(left_t[...], mine, preferred_element_type=F32)

    def pick(c):
        @pl.loop(0, blocks)
        def _(b):
            lanes = pl.ds(pl.multiple_of(b * BLOCK, BLOCK), BLOCK)
            got = jnp.dot(
                panels[c].reshape(2 * RK, W),
                hot[c * W : (c + 1) * W, lanes],
                preferred_element_type=F32,
            )
            lefts = lsel[:, lanes]
            real = jnp.sum(lefts * got, axis=0, keepdims=True)
            imag = jnp.sum(lefts[:RK] * got[RK:] - lefts[RK:] * got[:RK], axis=0, keepdims=True)
            if c == 0:
                acc[0:1, lanes] = real
                acc[1:2, lanes] = imag
            else:
                acc[0:1, lanes] += real
                acc[1:2, lanes] += imag

    def keep(g):
        for i in range(GROUP // LANES):
            value = acc[0:2, i * LANES : (i + 1) * LANES].astype(BF).astype(F32)
            picks[g * (GROUP // LANES) + i, 0:2, :] = value

    def multiply(c):
        @pl.loop(0, SW // 128)
        def _(b):
            rows = pl.ds(pl.multiple_of(b * 128, 128), 128)
            right = panels[c].reshape(2 * RK, W)
            stage[c, 0, rows, :] = jnp.dot(
                left_a[rows, :], right, preferred_element_type=F32
            ).astype(BF)
            stage[c, 1, rows, :] = jnp.dot(
                left_b[rows, :], right, preferred_element_type=F32
            ).astype(BF)

        out_copy(c).start()

    def out_copy(c):
        return pltpu.make_async_copy(
            stage.at[c], out_hbm.at[0, :, :, pl.ds(c * W, W)], out_sem.at[c]
        )

    picks[...] = jnp.zeros_like(picks)
    prepare(0)
    for c in range(CHUNKS):
        for n, (dp, dr) in enumerate(offsets):
            sender = lax.rem(pan + PAN - dp, PAN) * REP + lax.rem(rep + REP - dr, REP)
            panel_copy(n, c, sender).wait_recv()
        pick(c)
        if c < CHUNKS - 1:
            multiply(c)
    keep(0)

    @pl.loop(1, (NF * R * TL) // GROUP)
    def _(g):
        prepare(g)
        for c in range(CHUNKS):
            pick(c)
        keep(g)

    def pick_copy(k, target, slot):
        return pltpu.make_async_remote_copy(
            src_ref=picks.at[lax.div(target, PB)],
            dst_ref=arrived.at[slot],
            send_sem=pick_send.at[k],
            recv_sem=pick_recv.at[k],
            device_id=place(target),
            device_id_type=MESH,
        )

    @pl.loop(1, N)
    def _(k):
        pick_copy(k, lax.rem(me + k, N), me).start()

    arrived[me] = picks[lax.div(me, PB)]
    multiply(CHUNKS - 1)

    @pl.loop(1, N)
    def _(k):
        pick_copy(k, lax.rem(me + k, N), lax.rem(me + N - k, N)).wait_recv()

    for j in range(NF):
        total = arrived[j * R]
        for r in range(1, R):
            total = total + arrived[j * R + r]
        tidy[j : j + 1, :] = total[0:1]
        tidy[NF + j : NF + j + 1, :] = total[1:2]
    part = lax.rem(me, PB)
    value = tidy[:, :TL]
    for h in range(1, PB):
        value = jnp.where(part == h, tidy[:, h * TL : (h + 1) * TL], value)
    prim_v[...] = spectrum.astype(F32)[: 2 * NF] - value

    @pl.loop(1, N)
    def _(k):
        pick_copy(k, lax.rem(me + k, N), me).wait_send()

    for c in range(CHUNKS):
        for n in range(R - 1):
            panel_copy(n, c, reader).wait_send()
        out_copy(c).wait()


def local(traces, data, trace_shot, trace_recv, aper_panel, aper_order, aper_count):
    NF = lax.axis_size("freq") * data.shape[0]
    PAN, REP = lax.axis_size("pan"), lax.axis_size("rep")
    R = PAN * REP
    N = NF * R
    SW, NS = data.shape[2], data.shape[3]
    TL, NT = traces.shape
    total = trace_shot.shape[0]
    GROUP = min(total, 1024)
    W = NS // CHUNKS
    RK = R * KB
    table = jnp.asarray(spectral_table(NT, NF, FBIN0, FSTEP))
    sizes = (NF, PAN, REP, SW, NS, TL, GROUP)
    vmem = pl.BlockSpec(memory_space=pltpu.VMEM)
    smem = pl.BlockSpec(memory_space=pltpu.SMEM)
    hbm = pl.BlockSpec(memory_space=pl.ANY)
    multiples, primaries = pl.pallas_call(
        functools.partial(kernel, sizes),
        out_shape=(
            jax.ShapeDtypeStruct((1, 2, SW, NS), BF),
            jax.ShapeDtypeStruct((2 * NF, TL), F32),
        ),
        in_specs=[hbm, hbm, hbm, smem, smem, smem, vmem, vmem],
        out_specs=(hbm, vmem),
        scratch_shapes=[
            pltpu.VMEM((2, SW // KB, KB, NS), BF),
            pltpu.VMEM((TL, NT), BF),
            pltpu.VMEM(table.shape, BF),
            pltpu.VMEM((R - 1, CHUNKS, 2, KB, W), BF),
            pltpu.VMEM((CHUNKS, 2, R, KB, W), BF),
            pltpu.VMEM((NS, RK), BF),
            pltpu.VMEM((SW, 2 * RK), BF),
            pltpu.VMEM((SW, 2 * RK), BF),
            pltpu.VMEM((2 * RK, SW), BF),
            pltpu.VMEM((NS, GROUP), BF),
            pltpu.VMEM((2 * RK, GROUP), F32),
            pltpu.VMEM((8, GROUP), F32),
            pltpu.VMEM((total // LANES, 8, LANES), F32),
            pltpu.VMEM((N, 8, LANES), F32),
            pltpu.VMEM((2 * NF, LANES), F32),
            pltpu.VMEM((CHUNKS, 2, SW, W), BF),
            pltpu.SemaphoreType.DMA((3,)),
            pltpu.SemaphoreType.DMA((R - 1, CHUNKS)),
            pltpu.SemaphoreType.DMA((R - 1, CHUNKS)),
            pltpu.SemaphoreType.DMA((N,)),
            pltpu.SemaphoreType.DMA((N,)),
            pltpu.SemaphoreType.DMA((CHUNKS,)),
        ],
        compiler_params=pltpu.CompilerParams(
            collective_id=0, has_side_effects=True, vmem_limit_bytes=48 * 1024 * 1024
        ),
    )(
        data.reshape(1, 2, SW // KB, KB, NS),
        traces,
        table,
        aper_panel,
        aper_order,
        aper_count,
        trace_shot.reshape(-1, LANES),
        trace_recv.reshape(-1, LANES),
    )
    return multiples, jnp.transpose(primaries.reshape(2, NF, TL), (2, 0, 1))


def solution(mesh):
    in_specs = (
        P(("parts", "freq", "pan", "rep"), None),
        P(("parts", "freq"), None, ("pan", "rep"), None),
        P("parts"),
        P("parts"),
        P("parts", None),
        P("parts", None),
        P("parts"),
    )
    out_specs = (
        P(("parts", "freq"), None, ("pan", "rep"), None),
        P(("parts", "freq", "pan", "rep"), None, None),
    )
    return jax.shard_map(local, mesh=mesh, in_specs=in_specs, out_specs=out_specs, check_vma=False)
```

```python
import functools
import math

import jax
import jax.numpy as jnp
import numpy as np
from jax import lax
from jax.experimental import pallas as pl
from jax.experimental.pallas import tpu as pltpu
from jax.sharding import PartitionSpec as P

KB = 32
FBIN0 = 64
FSTEP = 3
LANES = 128
CHUNKS = 4
BLOCK = 2 * LANES
MESH = pl.DeviceIdType.MESH
BF = jnp.bfloat16
F32 = jnp.float32


def spectral_table(samples, count, first, stride):
    times = np.arange(samples, dtype=np.int32)
    bins = first + stride * np.arange(count, dtype=np.int32)
    phase = bins[:, None] * times[None, :] % samples
    angle = phase.astype(np.float32) * np.float32(2.0 * math.pi / samples)
    factor = np.float32(1.0 / math.sqrt(samples))
    rows = np.concatenate([np.cos(angle) * factor, -np.sin(angle) * factor], axis=0)
    padded = np.zeros((-(-rows.shape[0] // 16) * 16, samples), np.float32)
    padded[: rows.shape[0]] = rows
    return padded.astype(jnp.bfloat16)


def kernel(
    sizes,
    data_hbm, traces_hbm, table_hbm, panel_hbm, order_hbm, count_hbm, shot_hbm, recv_hbm,
    out_hbm, prim_v,
    panel_s, order_s, count_s, shot_v, recv_v, data_v, traces_v, table_v, send, panels, sel, left_a, left_b, left_t, hot, lsel, acc, picks,
    arrived, tidy, stage,
    load_sem, send_sem, recv_sem, pick_send, pick_recv, out_sem,
):
    NF, PAN, REP, SW, NS, TL, GROUP = sizes
    R = PAN * REP
    N = NF * R
    RK = R * KB
    W = NS // CHUNKS
    PB = LANES // TL
    freq, pan, rep = lax.axis_index("freq"), lax.axis_index("pan"), lax.axis_index("rep")
    reader = pan * REP + rep
    me = freq * R + reader

    def place(s):
        r = lax.rem(s, R)
        return {"freq": lax.div(s, R), "pan": lax.div(r, REP), "rep": lax.rem(r, REP)}

    loads = [
        pltpu.make_async_copy(panel_hbm, panel_s, load_sem.at[0]),
        pltpu.make_async_copy(data_hbm.at[0], data_v, load_sem.at[1]),
        pltpu.make_async_copy(order_hbm, order_s, load_sem.at[2]),
        pltpu.make_async_copy(count_hbm, count_s, load_sem.at[3]),
        pltpu.make_async_copy(shot_hbm, shot_v, load_sem.at[4]),
        pltpu.make_async_copy(recv_hbm, recv_v, load_sem.at[5]),
        pltpu.make_async_copy(traces_hbm, traces_v, load_sem.at[6]),
        pltpu.make_async_copy(table_hbm, table_v, load_sem.at[7]),
    ]
    for copy in loads:
        copy.start()

    barrier = pltpu.get_barrier_semaphore()

    @pl.loop(1, N)
    def _(k):
        pl.semaphore_signal(
            barrier, inc=1, device_id=place(lax.rem(me + k, N)), device_id_type=MESH
        )

    loads[0].wait()
    loads[1].wait()
    offsets = [(dp, dr) for dp in range(PAN) for dr in range(REP) if (dp, dr) != (0, 0)]
    offsets = [o for o in offsets if o[0]] + [o for o in offsets if not o[0]]

    for n, (dp, dr) in enumerate(offsets):
        p = panel_s[lax.rem(pan + dp, PAN) * REP + lax.rem(rep + dr, REP), reader]
        for c in range(CHUNKS):
            send[n, c] = data_v[:, p, :, c * W : (c + 1) * W]
    pl.semaphore_wait(barrier, N - 1)

    def panel_copy(n, c, slot):
        dp, dr = offsets[n]
        return pltpu.make_async_remote_copy(
            src_ref=send.at[n, c],
            dst_ref=panels.at[c, :, slot],
            send_sem=send_sem.at[n, c],
            recv_sem=recv_sem.at[n, c],
            device_id={"pan": lax.rem(pan + dp, PAN), "rep": lax.rem(rep + dr, REP)},
            device_id_type=MESH,
        )

    for c in range(CHUNKS):
        for n in range(R - 1):
            panel_copy(n, c, reader).start()
    p = panel_s[reader, reader]
    for c in range(CHUNKS):
        panels[c, :, reader] = data_v[:, p, :, c * W : (c + 1) * W]

    loads[2].wait()
    loads[3].wait()
    lane = lax.broadcasted_iota(jnp.int32, (1, RK), 1)
    column = jnp.full((1, RK), -1, jnp.int32)
    for q in range(R):
        hit = jnp.int32(0)
        for m in range(R):
            named = (order_s[reader, m] == q).astype(jnp.int32)
            hit = hit + named * (count_s[reader] > m).astype(jnp.int32)
        base = hit * (q * SW + panel_s[reader, q] * KB - q * KB + 2 * NS) - 2 * NS
        column = jnp.where((lane >= q * KB) & (lane < (q + 1) * KB), lane + base, column)

    @pl.loop(0, NS // 256)
    def _(b):
        at = pl.multiple_of(b * 256, 256)
        rows = lax.broadcasted_iota(jnp.int32, (256, RK), 0) + at
        sel[pl.ds(at, 256), :] = jnp.where(rows == column, 1.0, 0.0).astype(BF)

    @pl.loop(0, SW // 128)
    def _(b):
        rows = pl.ds(pl.multiple_of(b * 128, 128), 128)
        strips = pl.ds(b * (128 // KB), 128 // KB)
        real = jnp.dot(
            data_v[0, strips].reshape(128, NS), sel[...], preferred_element_type=F32
        )
        imag = jnp.dot(
            data_v[1, strips].reshape(128, NS), sel[...], preferred_element_type=F32
        )
        left_a[rows, :RK] = real.astype(BF)
        left_a[rows, RK:] = (-imag).astype(BF)
        left_b[rows, :RK] = imag.astype(BF)
        left_b[rows, RK:] = real.astype(BF)

    left_t[...] = left_a[...].T

    for copy in loads[4:]:
        copy.wait()
    spectrum = lax.dot_general(
        table_v[...], traces_v[...], (((1,), (1,)), ((), ())), preferred_element_type=F32
    ).astype(BF)

    blocks = GROUP // BLOCK

    def prepare(g):
        @pl.loop(0, blocks)
        def _(b):
            lanes = pl.ds(pl.multiple_of(b * BLOCK, BLOCK), BLOCK)
            row = (g * blocks + b) * 2
            recv = jnp.concatenate([recv_v[pl.ds(row, 1), :], recv_v[pl.ds(row + 1, 1), :]], axis=1)
            shot = jnp.concatenate([shot_v[pl.ds(row, 1), :], shot_v[pl.ds(row + 1, 1), :]], axis=1)
            for c in range(NS // 256):
                rows = lax.broadcasted_iota(jnp.int32, (256, BLOCK), 0) + c * 256
                hot[c * 256 : (c + 1) * 256, lanes] = jnp.where(rows == recv, 1.0, 0.0).astype(BF)
            mine = lax.broadcasted_iota(jnp.int32, (SW, BLOCK), 0) + reader * SW
            mine = jnp.where(mine == shot, 1.0, 0.0).astype(BF)
            lsel[:, lanes] = jnp.dot(left_t[...], mine, preferred_element_type=F32)

    def pick(c):
        @pl.loop(0, blocks)
        def _(b):
            lanes = pl.ds(pl.multiple_of(b * BLOCK, BLOCK), BLOCK)
            got = jnp.dot(
                panels[c].reshape(2 * RK, W),
                hot[c * W : (c + 1) * W, lanes],
                preferred_element_type=F32,
            )
            lefts = lsel[:, lanes]
            real = jnp.sum(lefts * got, axis=0, keepdims=True)
            imag = jnp.sum(lefts[:RK] * got[RK:] - lefts[RK:] * got[:RK], axis=0, keepdims=True)
            if c == 0:
                acc[0:1, lanes] = real
                acc[1:2, lanes] = imag
            else:
                acc[0:1, lanes] += real
                acc[1:2, lanes] += imag

    def keep(g):
        for i in range(GROUP // LANES):
            value = acc[0:2, i * LANES : (i + 1) * LANES].astype(BF).astype(F32)
            picks[g * (GROUP // LANES) + i, 0:2, :] = value

    def multiply(c):
        @pl.loop(0, SW // 128)
        def _(b):
            rows = pl.ds(pl.multiple_of(b * 128, 128), 128)
            right = panels[c].reshape(2 * RK, W)
            stage[c, 0, rows, :] = jnp.dot(
                left_a[rows, :], right, preferred_element_type=F32
            ).astype(BF)
            stage[c, 1, rows, :] = jnp.dot(
                left_b[rows, :], right, preferred_element_type=F32
            ).astype(BF)

        out_copy(c).start()

    def out_copy(c):
        return pltpu.make_async_copy(
            stage.at[c], out_hbm.at[0, :, :, pl.ds(c * W, W)], out_sem.at[c]
        )

    picks[...] = jnp.zeros_like(picks)
    prepare(0)
    for c in range(CHUNKS):
        for n, (dp, dr) in enumerate(offsets):
            sender = lax.rem(pan + PAN - dp, PAN) * REP + lax.rem(rep + REP - dr, REP)
            panel_copy(n, c, sender).wait_recv()
        pick(c)
        if c < CHUNKS - 1:
            multiply(c)
    keep(0)

    @pl.loop(1, (NF * R * TL) // GROUP)
    def _(g):
        prepare(g)
        for c in range(CHUNKS):
            pick(c)
        keep(g)

    def pick_copy(k, target, slot):
        return pltpu.make_async_remote_copy(
            src_ref=picks.at[lax.div(target, PB)],
            dst_ref=arrived.at[slot],
            send_sem=pick_send.at[k],
            recv_sem=pick_recv.at[k],
            device_id=place(target),
            device_id_type=MESH,
        )

    @pl.loop(1, N)
    def _(k):
        pick_copy(k, lax.rem(me + k, N), me).start()

    arrived[me] = picks[lax.div(me, PB)]
    multiply(CHUNKS - 1)

    @pl.loop(1, N)
    def _(k):
        pick_copy(k, lax.rem(me + k, N), lax.rem(me + N - k, N)).wait_recv()

    for j in range(NF):
        total = arrived[j * R]
        for r in range(1, R):
            total = total + arrived[j * R + r]
        tidy[j : j + 1, :] = total[0:1]
        tidy[NF + j : NF + j + 1, :] = total[1:2]
    part = lax.rem(me, PB)
    value = tidy[:, :TL]
    for h in range(1, PB):
        value = jnp.where(part == h, tidy[:, h * TL : (h + 1) * TL], value)
    prim_v[...] = spectrum.astype(F32)[: 2 * NF] - value

    @pl.loop(1, N)
    def _(k):
        pick_copy(k, lax.rem(me + k, N), me).wait_send()

    for c in range(CHUNKS):
        for n in range(R - 1):
            panel_copy(n, c, reader).wait_send()
        out_copy(c).wait()


def local(traces, data, trace_shot, trace_recv, aper_panel, aper_order, aper_count):
    NF = lax.axis_size("freq") * data.shape[0]
    PAN, REP = lax.axis_size("pan"), lax.axis_size("rep")
    R = PAN * REP
    N = NF * R
    SW, NS = data.shape[2], data.shape[3]
    TL, NT = traces.shape
    total = trace_shot.shape[0]
    GROUP = min(total, 1024)
    W = NS // CHUNKS
    RK = R * KB
    table = jnp.asarray(spectral_table(NT, NF, FBIN0, FSTEP))
    sizes = (NF, PAN, REP, SW, NS, TL, GROUP)
    vmem = pl.BlockSpec(memory_space=pltpu.VMEM)
    hbm = pl.BlockSpec(memory_space=pltpu.HBM)
    anywhere = pl.BlockSpec(memory_space=pl.ANY)
    multiples, primaries = pl.pallas_call(
        functools.partial(kernel, sizes),
        out_shape=(
            jax.ShapeDtypeStruct((1, 2, SW, NS), BF),
            jax.ShapeDtypeStruct((2 * NF, TL), F32),
        ),
        in_specs=[hbm] * 8,
        out_specs=(anywhere, vmem),
        scratch_shapes=[
            pltpu.SMEM((R, R), jnp.int32),
            pltpu.SMEM((R, R), jnp.int32),
            pltpu.SMEM((R,), jnp.int32),
            pltpu.VMEM((total // LANES, LANES), jnp.int32),
            pltpu.VMEM((total // LANES, LANES), jnp.int32),
            pltpu.VMEM((2, SW // KB, KB, NS), BF),
            pltpu.VMEM((TL, NT), BF),
            pltpu.VMEM(table.shape, BF),
            pltpu.VMEM((R - 1, CHUNKS, 2, KB, W), BF),
            pltpu.VMEM((CHUNKS, 2, R, KB, W), BF),
            pltpu.VMEM((NS, RK), BF),
            pltpu.VMEM((SW, 2 * RK), BF),
            pltpu.VMEM((SW, 2 * RK), BF),
            pltpu.VMEM((2 * RK, SW), BF),
            pltpu.VMEM((NS, GROUP), BF),
            pltpu.VMEM((2 * RK, GROUP), F32),
            pltpu.VMEM((8, GROUP), F32),
            pltpu.VMEM((total // LANES, 8, LANES), F32),
            pltpu.VMEM((N, 8, LANES), F32),
            pltpu.VMEM((2 * NF, LANES), F32),
            pltpu.VMEM((CHUNKS, 2, SW, W), BF),
            pltpu.SemaphoreType.DMA((8,)),
            pltpu.SemaphoreType.DMA((R - 1, CHUNKS)),
            pltpu.SemaphoreType.DMA((R - 1, CHUNKS)),
            pltpu.SemaphoreType.DMA((N,)),
            pltpu.SemaphoreType.DMA((N,)),
            pltpu.SemaphoreType.DMA((CHUNKS,)),
        ],
        compiler_params=pltpu.CompilerParams(
            collective_id=0, has_side_effects=True, vmem_limit_bytes=48 * 1024 * 1024
        ),
    )(
        *(
            pltpu.with_memory_space_constraint(operand, pltpu.HBM)
            for operand in (
                data.reshape(1, 2, SW // KB, KB, NS),
                traces,
                table,
                aper_panel,
                aper_order,
                aper_count,
                trace_shot.reshape(-1, LANES),
                trace_recv.reshape(-1, LANES),
            )
        )
    )
    return multiples, jnp.transpose(primaries.reshape(2, NF, TL), (2, 0, 1))


def solution(mesh):
    in_specs = (
        P(("parts", "freq", "pan", "rep"), None),
        P(("parts", "freq"), None, ("pan", "rep"), None),
        P("parts"),
        P("parts"),
        P("parts", None),
        P("parts", None),
        P("parts"),
    )
    out_specs = (
        P(("parts", "freq"), None, ("pan", "rep"), None),
        P(("parts", "freq", "pan", "rep"), None, None),
    )
    return jax.shard_map(local, mesh=mesh, in_specs=in_specs, out_specs=out_specs, check_vma=False)
```

```python
import functools
import math

import jax
import jax.numpy as jnp
import numpy as np
from jax import lax
from jax.experimental import pallas as pl
from jax.experimental.pallas import tpu as pltpu
from jax.sharding import PartitionSpec as P

KB = 32
FBIN0 = 64
FSTEP = 3
LANES = 128
CHUNKS = 4
BLOCK = 2 * LANES
MESH = pl.DeviceIdType.MESH
BF = jnp.bfloat16
F32 = jnp.float32


def spectral_table(samples, count, first, stride):
    times = np.arange(samples, dtype=np.int32)
    bins = first + stride * np.arange(count, dtype=np.int32)
    phase = bins[:, None] * times[None, :] % samples
    angle = phase.astype(np.float32) * np.float32(2.0 * math.pi / samples)
    factor = np.float32(1.0 / math.sqrt(samples))
    rows = np.concatenate([np.cos(angle) * factor, -np.sin(angle) * factor], axis=0)
    padded = np.zeros((-(-rows.shape[0] // 16) * 16, samples), np.float32)
    padded[: rows.shape[0]] = rows
    return padded.astype(jnp.bfloat16)


def kernel(
    sizes,
    data_hbm, traces_hbm, table_hbm, panel_hbm, order_hbm, count_hbm, shot_hbm, recv_hbm,
    out_hbm, prim_v,
    panel_s, order_s, count_s, shot_v, recv_v, data_v, traces_v, table_v, send, panels, sel, left_a, left_b, left_t, hot, lsel, acc, picks,
    arrived, tidy, stage,
    load_sem, send_sem, recv_sem, pick_send, pick_recv, out_sem, up_sem, down_sem, all_sem,
):
    NF, PAN, REP, SW, NS, TL, GROUP = sizes
    R = PAN * REP
    N = NF * R
    RK = R * KB
    W = NS // CHUNKS
    PB = LANES // TL
    freq, pan, rep = lax.axis_index("freq"), lax.axis_index("pan"), lax.axis_index("rep")
    reader = pan * REP + rep
    me = freq * R + reader

    def turn(at, step, size):
        return at if isinstance(step, int) and step == 0 else lax.rem(at + step, size)

    pans = [turn(pan, k, PAN) for k in range(PAN)]
    reps = [turn(rep, k, REP) for k in range(REP)]
    back_pans = [turn(pan, PAN - k, PAN) if k else pan for k in range(PAN)]
    back_reps = [turn(rep, REP - k, REP) if k else rep for k in range(REP)]

    def each_peer(act):
        def band(k):
            there = turn(freq, k, NF)
            back = freq if isinstance(k, int) and k == 0 else lax.rem(freq + NF - k, NF)
            for dp in range(PAN):
                for dr in range(REP):
                    if isinstance(k, int) and (k, dp, dr) == (0, 0, 0):
                        continue
                    act(
                        k * R + dp * REP + dr,
                        (there, pans[dp], reps[dr]),
                        (back, back_pans[dp], back_reps[dr]),
                    )

        band(0)
        if N <= 32:
            for k in range(1, NF):
                band(k)
        else:
            pl.loop(1, NF)(band)

    def place(spot):
        return {"freq": spot[0], "pan": spot[1], "rep": spot[2]}

    def number(spot):
        return spot[0] * R + spot[1] * REP + spot[2]

    def lane_block(spot):
        return spot[0] * PAN + spot[1] if REP == PB else lax.div(number(spot), PB)

    loads = [
        pltpu.make_async_copy(panel_hbm, panel_s, load_sem.at[0]),
        pltpu.make_async_copy(data_hbm.at[0], data_v, load_sem.at[1]),
        pltpu.make_async_copy(order_hbm, order_s, load_sem.at[2]),
        pltpu.make_async_copy(count_hbm, count_s, load_sem.at[3]),
        pltpu.make_async_copy(shot_hbm, shot_v, load_sem.at[4]),
        pltpu.make_async_copy(recv_hbm, recv_v, load_sem.at[5]),
        pltpu.make_async_copy(traces_hbm, traces_v, load_sem.at[6]),
        pltpu.make_async_copy(table_hbm, table_v, load_sem.at[7]),
    ]
    for copy in loads:
        copy.start()

    barrier = pltpu.get_barrier_semaphore()

    offsets = [(dp, dr) for dp in range(PAN) for dr in range(REP) if (dp, dr) != (0, 0)]
    offsets = [o for o in offsets if o[0]] + [o for o in offsets if not o[0]]
    gate = reader == 0
    above, below = gate & (freq > 0), gate & (freq < NF - 1)

    def tell(sem, **where):
        pl.semaphore_signal(sem, inc=1, device_id=where, device_id_type=MESH)

    for dp, dr in offsets:
        tell(barrier, pan=pans[dp], rep=reps[dr])
    pl.when(above)(lambda: tell(barrier, freq=freq - 1))
    pl.when(below)(lambda: tell(barrier, freq=freq + 1))

    def send_up():
        tell(up_sem, freq=freq + 1)

    def send_down():
        tell(down_sem, freq=freq - 1)

    def pass_up():
        pl.semaphore_wait(up_sem, 1)
        send_up()

    def pass_down():
        pl.semaphore_wait(down_sem, 1)
        send_down()

    loads[0].wait()
    loads[1].wait()
    for n, (dp, dr) in enumerate(offsets):
        p = panel_s[pans[dp] * REP + reps[dr], reader]
        for c in range(CHUNKS):
            send[n, c] = data_v[:, p, :, c * W : (c + 1) * W]
    bands_beside = lax.div(freq + NF - 1, NF) + 1 - lax.div(freq + 1, NF)
    pl.semaphore_wait(barrier, R - 1 + (1 - lax.div(reader + R - 1, R)) * bands_beside)

    def panel_copy(n, c, slot):
        dp, dr = offsets[n]
        return pltpu.make_async_remote_copy(
            src_ref=send.at[n, c],
            dst_ref=panels.at[c, :, slot],
            send_sem=send_sem.at[n, c],
            recv_sem=recv_sem.at[n, c],
            device_id={"pan": pans[dp], "rep": reps[dr]},
            device_id_type=MESH,
        )

    for c in range(CHUNKS):
        for n in range(R - 1):
            panel_copy(n, c, reader).start()
    pl.when(gate & (freq == 0))(send_up)
    pl.when(gate & (freq == NF - 1))(send_down)
    p = panel_s[reader, reader]
    for c in range(CHUNKS):
        panels[c, :, reader] = data_v[:, p, :, c * W : (c + 1) * W]

    loads[2].wait()
    loads[3].wait()
    lane = lax.broadcasted_iota(jnp.int32, (1, RK), 1)
    column = jnp.full((1, RK), -1, jnp.int32)
    for q in range(R):
        hit = jnp.int32(0)
        for m in range(R):
            named = (order_s[reader, m] == q).astype(jnp.int32)
            hit = hit + named * (count_s[reader] > m).astype(jnp.int32)
        base = hit * (q * SW + panel_s[reader, q] * KB - q * KB + 2 * NS) - 2 * NS
        column = jnp.where((lane >= q * KB) & (lane < (q + 1) * KB), lane + base, column)

    @pl.loop(0, NS // 256)
    def _(b):
        at = pl.multiple_of(b * 256, 256)
        rows = lax.broadcasted_iota(jnp.int32, (256, RK), 0) + at
        sel[pl.ds(at, 256), :] = jnp.where(rows == column, 1.0, 0.0).astype(BF)

    @pl.loop(0, SW // 128)
    def _(b):
        rows = pl.ds(pl.multiple_of(b * 128, 128), 128)
        strips = pl.ds(b * (128 // KB), 128 // KB)
        real = jnp.dot(
            data_v[0, strips].reshape(128, NS), sel[...], preferred_element_type=F32
        )
        imag = jnp.dot(
            data_v[1, strips].reshape(128, NS), sel[...], preferred_element_type=F32
        )
        left_a[rows, :RK] = real.astype(BF)
        left_a[rows, RK:] = (-imag).astype(BF)
        left_b[rows, :RK] = imag.astype(BF)
        left_b[rows, RK:] = real.astype(BF)

    left_t[...] = left_a[...].T

    for copy in loads[4:]:
        copy.wait()
    spectrum = lax.dot_general(
        table_v[...], traces_v[...], (((1,), (1,)), ((), ())), preferred_element_type=F32
    ).astype(BF)

    pl.when(gate & (freq == 1))(pass_up)
    pl.when(gate & (freq == NF - 2))(pass_down)

    blocks = GROUP // BLOCK

    def prepare(g):
        @pl.loop(0, blocks)
        def _(b):
            lanes = pl.ds(pl.multiple_of(b * BLOCK, BLOCK), BLOCK)
            row = (g * blocks + b) * 2
            recv = jnp.concatenate([recv_v[pl.ds(row, 1), :], recv_v[pl.ds(row + 1, 1), :]], axis=1)
            shot = jnp.concatenate([shot_v[pl.ds(row, 1), :], shot_v[pl.ds(row + 1, 1), :]], axis=1)
            for c in range(NS // 256):
                rows = lax.broadcasted_iota(jnp.int32, (256, BLOCK), 0) + c * 256
                hot[c * 256 : (c + 1) * 256, lanes] = jnp.where(rows == recv, 1.0, 0.0).astype(BF)
            mine = lax.broadcasted_iota(jnp.int32, (SW, BLOCK), 0) + reader * SW
            mine = jnp.where(mine == shot, 1.0, 0.0).astype(BF)
            lsel[:, lanes] = jnp.dot(left_t[...], mine, preferred_element_type=F32)

    def pick(c):
        @pl.loop(0, blocks)
        def _(b):
            lanes = pl.ds(pl.multiple_of(b * BLOCK, BLOCK), BLOCK)
            got = jnp.dot(
                panels[c].reshape(2 * RK, W),
                hot[c * W : (c + 1) * W, lanes],
                preferred_element_type=F32,
            )
            lefts = lsel[:, lanes]
            real = jnp.sum(lefts * got, axis=0, keepdims=True)
            imag = jnp.sum(lefts[:RK] * got[RK:] - lefts[RK:] * got[:RK], axis=0, keepdims=True)
            if c == 0:
                acc[0:1, lanes] = real
                acc[1:2, lanes] = imag
            else:
                acc[0:1, lanes] += real
                acc[1:2, lanes] += imag

    def keep(g):
        for i in range(GROUP // LANES):
            value = acc[0:2, i * LANES : (i + 1) * LANES].astype(BF).astype(F32)
            picks[g * (GROUP // LANES) + i, 0:2, :] = value

    def multiply(c):
        @pl.loop(0, SW // 128)
        def _(b):
            rows = pl.ds(pl.multiple_of(b * 128, 128), 128)
            right = panels[c].reshape(2 * RK, W)
            stage[c, 0, rows, :] = jnp.dot(
                left_a[rows, :], right, preferred_element_type=F32
            ).astype(BF)
            stage[c, 1, rows, :] = jnp.dot(
                left_b[rows, :], right, preferred_element_type=F32
            ).astype(BF)

        out_copy(c).start()

    def out_copy(c):
        return pltpu.make_async_copy(
            stage.at[c], out_hbm.at[0, :, :, pl.ds(c * W, W)], out_sem.at[c]
        )

    picks[...] = jnp.zeros_like(picks)
    prepare(0)
    pl.when(gate & (freq >= 2) & (freq <= NF - 2))(pass_up)
    pl.when(gate & (freq >= 1) & (freq <= NF - 3))(pass_down)
    for c in range(CHUNKS):
        for n, (dp, dr) in enumerate(offsets):
            sender = back_pans[dp] * REP + back_reps[dr]
            panel_copy(n, c, sender).wait_recv()
        pick(c)
        if c < CHUNKS - 1:
            multiply(c)
        if c == 1:

            @pl.when(gate)
            def _():
                pl.when(freq == NF - 1)(lambda: pl.semaphore_wait(up_sem, 1))
                pl.when(freq == 0)(lambda: pl.semaphore_wait(down_sem, 1))
                for dp, dr in offsets:
                    tell(all_sem, pan=pans[dp], rep=reps[dr])

    keep(0)
    pl.when(reader > 0)(lambda: pl.semaphore_wait(all_sem, 1))

    @pl.loop(1, (NF * R * TL) // GROUP)
    def _(g):
        prepare(g)
        for c in range(CHUNKS):
            pick(c)
        keep(g)

    def pick_copy(k, target, slot):
        return pltpu.make_async_remote_copy(
            src_ref=picks.at[lane_block(target)],
            dst_ref=arrived.at[slot],
            send_sem=pick_send.at[k],
            recv_sem=pick_recv.at[k],
            device_id=place(target),
            device_id_type=MESH,
        )

    each_peer(lambda k, target, source: pick_copy(k, target, me).start())
    arrived[me] = picks[lane_block((freq, pan, rep))]
    multiply(CHUNKS - 1)
    each_peer(lambda k, target, source: pick_copy(k, target, number(source)).wait_recv())

    for j in range(NF):
        total = arrived[j * R]
        for r in range(1, R):
            total = total + arrived[j * R + r]
        tidy[j : j + 1, :] = total[0:1]
        tidy[NF + j : NF + j + 1, :] = total[1:2]
    part = rep if REP == PB else lax.rem(me, PB)
    value = tidy[:, :TL]
    for h in range(1, PB):
        value = jnp.where(part == h, tidy[:, h * TL : (h + 1) * TL], value)
    prim_v[...] = spectrum.astype(F32)[: 2 * NF] - value

    each_peer(lambda k, target, source: pick_copy(k, target, me).wait_send())
    for c in range(CHUNKS):
        for n in range(R - 1):
            panel_copy(n, c, reader).wait_send()
        out_copy(c).wait()


def finish(multiples, primaries, multiples_out, primaries_out, sems):
    half = multiples.shape[2] // 2
    copies = []
    for part in range(2):
        for h in range(2):
            where = (0, part, slice(h * half, (h + 1) * half))
            copies.append(
                pltpu.make_async_copy(
                    multiples.at[where], multiples_out.at[where], sems.at[2 * part + h]
                )
            )
    for copy in copies:
        copy.start()
    count = primaries_out.shape[1]
    primaries_out[0] = primaries[:count]
    primaries_out[1] = primaries[count:]
    for copy in copies:
        copy.wait()


def local(traces, data, trace_shot, trace_recv, aper_panel, aper_order, aper_count):
    NF = lax.axis_size("freq") * data.shape[0]
    PAN, REP = lax.axis_size("pan"), lax.axis_size("rep")
    R = PAN * REP
    N = NF * R
    SW, NS = data.shape[2], data.shape[3]
    TL, NT = traces.shape
    total = trace_shot.shape[0]
    GROUP = min(total, 1024)
    W = NS // CHUNKS
    RK = R * KB
    table = jnp.asarray(spectral_table(NT, NF, FBIN0, FSTEP))
    sizes = (NF, PAN, REP, SW, NS, TL, GROUP)
    vmem = pl.BlockSpec(memory_space=pltpu.VMEM)
    hbm = pl.BlockSpec(memory_space=pltpu.HBM)
    anywhere = pl.BlockSpec(memory_space=pl.ANY)
    multiples, primaries = pl.pallas_call(
        functools.partial(kernel, sizes),
        out_shape=(
            jax.ShapeDtypeStruct((1, 2, SW, NS), BF),
            jax.ShapeDtypeStruct((2 * NF, TL), F32),
        ),
        in_specs=[hbm] * 8,
        out_specs=(anywhere, vmem),
        scratch_shapes=[
            pltpu.SMEM((R, R), jnp.int32),
            pltpu.SMEM((R, R), jnp.int32),
            pltpu.SMEM((R,), jnp.int32),
            pltpu.VMEM((total // LANES, LANES), jnp.int32),
            pltpu.VMEM((total // LANES, LANES), jnp.int32),
            pltpu.VMEM((2, SW // KB, KB, NS), BF),
            pltpu.VMEM((TL, NT), BF),
            pltpu.VMEM(table.shape, BF),
            pltpu.VMEM((R - 1, CHUNKS, 2, KB, W), BF),
            pltpu.VMEM((CHUNKS, 2, R, KB, W), BF),
            pltpu.VMEM((NS, RK), BF),
            pltpu.VMEM((SW, 2 * RK), BF),
            pltpu.VMEM((SW, 2 * RK), BF),
            pltpu.VMEM((2 * RK, SW), BF),
            pltpu.VMEM((NS, GROUP), BF),
            pltpu.VMEM((2 * RK, GROUP), F32),
            pltpu.VMEM((8, GROUP), F32),
            pltpu.VMEM((total // LANES, 8, LANES), F32),
            pltpu.VMEM((N, 8, LANES), F32),
            pltpu.VMEM((2 * NF, LANES), F32),
            pltpu.VMEM((CHUNKS, 2, SW, W), BF),
            pltpu.SemaphoreType.DMA((8,)),
            pltpu.SemaphoreType.DMA((R - 1, CHUNKS)),
            pltpu.SemaphoreType.DMA((R - 1, CHUNKS)),
            pltpu.SemaphoreType.DMA((N,)),
            pltpu.SemaphoreType.DMA((N,)),
            pltpu.SemaphoreType.DMA((CHUNKS,)),
            pltpu.SemaphoreType.REGULAR,
            pltpu.SemaphoreType.REGULAR,
            pltpu.SemaphoreType.REGULAR,
        ],
        compiler_params=pltpu.CompilerParams(
            collective_id=0, has_side_effects=True, vmem_limit_bytes=48 * 1024 * 1024
        ),
    )(
        *(
            pltpu.with_memory_space_constraint(operand, pltpu.HBM)
            for operand in (
                data.reshape(1, 2, SW // KB, KB, NS),
                traces,
                table,
                aper_panel,
                aper_order,
                aper_count,
                trace_shot.reshape(-1, LANES),
                trace_recv.reshape(-1, LANES),
            )
        )
    )
    multiples, primaries = pl.pallas_call(
        finish,
        out_shape=(
            jax.ShapeDtypeStruct((1, 2, SW, NS), BF),
            jax.ShapeDtypeStruct((2, NF, TL), F32),
        ),
        in_specs=[anywhere, vmem],
        out_specs=(hbm, vmem),
        scratch_shapes=[pltpu.SemaphoreType.DMA((4,))],
    )(multiples, primaries)
    return multiples, jnp.transpose(primaries, (2, 0, 1))


def solution(mesh):
    in_specs = (
        P(("parts", "freq", "pan", "rep"), None),
        P(("parts", "freq"), None, ("pan", "rep"), None),
        P("parts"),
        P("parts"),
        P("parts", None),
        P("parts", None),
        P("parts"),
    )
    out_specs = (
        P(("parts", "freq"), None, ("pan", "rep"), None),
        P(("parts", "freq", "pan", "rep"), None, None),
    )
    return jax.shard_map(local, mesh=mesh, in_specs=in_specs, out_specs=out_specs, check_vma=False)
```

```python
import functools
import math

import jax
import jax.numpy as jnp
import numpy as np
from jax import lax
from jax.experimental import pallas as pl
from jax.experimental.pallas import tpu as pltpu
from jax.sharding import PartitionSpec as P

KB = 32
FBIN0 = 64
FSTEP = 3
LANES = 128
CHUNKS = 4
BLOCK = 2 * LANES
MESH = pl.DeviceIdType.MESH
BF = jnp.bfloat16
F32 = jnp.float32


def spectral_table(samples, count, first, stride):
    times = np.arange(samples, dtype=np.int32)
    bins = first + stride * np.arange(count, dtype=np.int32)
    phase = bins[:, None] * times[None, :] % samples
    angle = phase.astype(np.float32) * np.float32(2.0 * math.pi / samples)
    factor = np.float32(1.0 / math.sqrt(samples))
    rows = np.concatenate([np.cos(angle) * factor, -np.sin(angle) * factor], axis=0)
    padded = np.zeros((-(-rows.shape[0] // 16) * 16, samples), np.float32)
    padded[: rows.shape[0]] = rows
    return padded.astype(jnp.bfloat16)


def kernel(
    sizes,
    data_hbm, traces_hbm, table_hbm, panel_hbm, order_hbm, count_hbm, shot_hbm, recv_hbm,
    out_hbm, prim_v,
    panel_s, order_s, count_s, shot_v, recv_v, data_v, traces_v, table_v, send, panels, sel, left_a, left_b, left_t, hot, lsel, acc, picks,
    arrived, tidy, stage,
    load_sem, send_sem, recv_sem, pick_send, pick_recv, out_sem,
):
    NF, PAN, REP, SW, NS, TL, GROUP = sizes
    R = PAN * REP
    N = NF * R
    RK = R * KB
    W = NS // CHUNKS
    PB = LANES // TL
    freq, pan, rep = lax.axis_index("freq"), lax.axis_index("pan"), lax.axis_index("rep")
    reader = pan * REP + rep
    me = freq * R + reader

    def turn(at, step, size):
        return at if isinstance(step, int) and step == 0 else lax.rem(at + step, size)

    pans = [turn(pan, k, PAN) for k in range(PAN)]
    reps = [turn(rep, k, REP) for k in range(REP)]
    back_pans = [turn(pan, PAN - k, PAN) if k else pan for k in range(PAN)]
    back_reps = [turn(rep, REP - k, REP) if k else rep for k in range(REP)]

    def each_peer(act):
        def band(k):
            there = turn(freq, k, NF)
            back = freq if isinstance(k, int) and k == 0 else lax.rem(freq + NF - k, NF)
            for dp in range(PAN):
                for dr in range(REP):
                    if isinstance(k, int) and (k, dp, dr) == (0, 0, 0):
                        continue
                    act(
                        k * R + dp * REP + dr,
                        (there, pans[dp], reps[dr]),
                        (back, back_pans[dp], back_reps[dr]),
                    )

        band(0)
        if N <= 32:
            for k in range(1, NF):
                band(k)
        else:
            pl.loop(1, NF)(band)

    def place(spot):
        return {"freq": spot[0], "pan": spot[1], "rep": spot[2]}

    def number(spot):
        return spot[0] * R + spot[1] * REP + spot[2]

    def lane_block(spot):
        return spot[0] * PAN + spot[1] if REP == PB else lax.div(number(spot), PB)

    loads = [
        pltpu.make_async_copy(panel_hbm, panel_s, load_sem.at[0]),
        pltpu.make_async_copy(data_hbm.at[0], data_v, load_sem.at[1]),
        pltpu.make_async_copy(order_hbm, order_s, load_sem.at[2]),
        pltpu.make_async_copy(count_hbm, count_s, load_sem.at[3]),
        pltpu.make_async_copy(shot_hbm, shot_v, load_sem.at[4]),
        pltpu.make_async_copy(recv_hbm, recv_v, load_sem.at[5]),
        pltpu.make_async_copy(traces_hbm, traces_v, load_sem.at[6]),
        pltpu.make_async_copy(table_hbm, table_v, load_sem.at[7]),
    ]
    for copy in loads:
        copy.start()

    barrier = pltpu.get_barrier_semaphore()

    each_peer(
        lambda k, target, source: pl.semaphore_signal(
            barrier, inc=1, device_id=place(target), device_id_type=MESH
        )
    )

    loads[0].wait()
    loads[1].wait()
    offsets = [(dp, dr) for dp in range(PAN) for dr in range(REP) if (dp, dr) != (0, 0)]
    offsets = [o for o in offsets if o[0]] + [o for o in offsets if not o[0]]

    for n, (dp, dr) in enumerate(offsets):
        p = panel_s[pans[dp] * REP + reps[dr], reader]
        for c in range(CHUNKS):
            send[n, c] = data_v[:, p, :, c * W : (c + 1) * W]
    pl.semaphore_wait(barrier, N - 1)

    def panel_copy(n, c, slot):
        dp, dr = offsets[n]
        return pltpu.make_async_remote_copy(
            src_ref=send.at[n, c],
            dst_ref=panels.at[c, :, slot],
            send_sem=send_sem.at[n, c],
            recv_sem=recv_sem.at[n, c],
            device_id={"pan": pans[dp], "rep": reps[dr]},
            device_id_type=MESH,
        )

    for c in range(CHUNKS):
        for n in range(R - 1):
            panel_copy(n, c, reader).start()
    p = panel_s[reader, reader]
    for c in range(CHUNKS):
        panels[c, :, reader] = data_v[:, p, :, c * W : (c + 1) * W]

    loads[2].wait()
    loads[3].wait()
    lane = lax.broadcasted_iota(jnp.int32, (1, RK), 1)
    column = jnp.full((1, RK), -1, jnp.int32)
    for q in range(R):
        hit = jnp.int32(0)
        for m in range(R):
            named = (order_s[reader, m] == q).astype(jnp.int32)
            hit = hit + named * (count_s[reader] > m).astype(jnp.int32)
        base = hit * (q * SW + panel_s[reader, q] * KB - q * KB + 2 * NS) - 2 * NS
        column = jnp.where((lane >= q * KB) & (lane < (q + 1) * KB), lane + base, column)

    @pl.loop(0, NS // 256)
    def _(b):
        at = pl.multiple_of(b * 256, 256)
        rows = lax.broadcasted_iota(jnp.int32, (256, RK), 0) + at
        sel[pl.ds(at, 256), :] = jnp.where(rows == column, 1.0, 0.0).astype(BF)

    @pl.loop(0, SW // 128)
    def _(b):
        rows = pl.ds(pl.multiple_of(b * 128, 128), 128)
        strips = pl.ds(b * (128 // KB), 128 // KB)
        real = jnp.dot(
            data_v[0, strips].reshape(128, NS), sel[...], preferred_element_type=F32
        )
        imag = jnp.dot(
            data_v[1, strips].reshape(128, NS), sel[...], preferred_element_type=F32
        )
        left_a[rows, :RK] = real.astype(BF)
        left_a[rows, RK:] = (-imag).astype(BF)
        left_b[rows, :RK] = imag.astype(BF)
        left_b[rows, RK:] = real.astype(BF)

    left_t[...] = left_a[...].T

    for copy in loads[4:]:
        copy.wait()
    spectrum = lax.dot_general(
        table_v[...], traces_v[...], (((1,), (1,)), ((), ())), preferred_element_type=F32
    ).astype(BF)

    blocks = GROUP // BLOCK

    def prepare(g):
        @pl.loop(0, blocks)
        def _(b):
            lanes = pl.ds(pl.multiple_of(b * BLOCK, BLOCK), BLOCK)
            row = (g * blocks + b) * 2
            recv = jnp.concatenate([recv_v[pl.ds(row, 1), :], recv_v[pl.ds(row + 1, 1), :]], axis=1)
            shot = jnp.concatenate([shot_v[pl.ds(row, 1), :], shot_v[pl.ds(row + 1, 1), :]], axis=1)
            for c in range(NS // 256):
                rows = lax.broadcasted_iota(jnp.int32, (256, BLOCK), 0) + c * 256
                hot[c * 256 : (c + 1) * 256, lanes] = jnp.where(rows == recv, 1.0, 0.0).astype(BF)
            mine = lax.broadcasted_iota(jnp.int32, (SW, BLOCK), 0) + reader * SW
            mine = jnp.where(mine == shot, 1.0, 0.0).astype(BF)
            lsel[:, lanes] = jnp.dot(left_t[...], mine, preferred_element_type=F32)

    def pick(c):
        @pl.loop(0, blocks)
        def _(b):
            lanes = pl.ds(pl.multiple_of(b * BLOCK, BLOCK), BLOCK)
            got = jnp.dot(
                panels[c].reshape(2 * RK, W),
                hot[c * W : (c + 1) * W, lanes],
                preferred_element_type=F32,
            )
            lefts = lsel[:, lanes]
            real = jnp.sum(lefts * got, axis=0, keepdims=True)
            imag = jnp.sum(lefts[:RK] * got[RK:] - lefts[RK:] * got[:RK], axis=0, keepdims=True)
            if c == 0:
                acc[0:1, lanes] = real
                acc[1:2, lanes] = imag
            else:
                acc[0:1, lanes] += real
                acc[1:2, lanes] += imag

    def keep(g):
        for i in range(GROUP // LANES):
            value = acc[0:2, i * LANES : (i + 1) * LANES].astype(BF).astype(F32)
            picks[g * (GROUP // LANES) + i, 0:2, :] = value

    def multiply(c):
        @pl.loop(0, SW // 128)
        def _(b):
            rows = pl.ds(pl.multiple_of(b * 128, 128), 128)
            right = panels[c].reshape(2 * RK, W)
            stage[c, 0, rows, :] = jnp.dot(
                left_a[rows, :], right, preferred_element_type=F32
            ).astype(BF)
            stage[c, 1, rows, :] = jnp.dot(
                left_b[rows, :], right, preferred_element_type=F32
            ).astype(BF)

        out_copy(c).start()

    def out_copy(c):
        return pltpu.make_async_copy(
            stage.at[c], out_hbm.at[0, :, :, pl.ds(c * W, W)], out_sem.at[c]
        )

    picks[...] = jnp.zeros_like(picks)
    prepare(0)
    for c in range(CHUNKS):
        for n, (dp, dr) in enumerate(offsets):
            sender = back_pans[dp] * REP + back_reps[dr]
            panel_copy(n, c, sender).wait_recv()
        pick(c)
        if c < CHUNKS - 1:
            multiply(c)
    keep(0)

    @pl.loop(1, (NF * R * TL) // GROUP)
    def _(g):
        prepare(g)
        for c in range(CHUNKS):
            pick(c)
        keep(g)

    def pick_copy(k, target, slot):
        return pltpu.make_async_remote_copy(
            src_ref=picks.at[lane_block(target)],
            dst_ref=arrived.at[slot],
            send_sem=pick_send.at[k],
            recv_sem=pick_recv.at[k],
            device_id=place(target),
            device_id_type=MESH,
        )

    each_peer(lambda k, target, source: pick_copy(k, target, me).start())
    arrived[me] = picks[lane_block((freq, pan, rep))]
    multiply(CHUNKS - 1)
    each_peer(lambda k, target, source: pick_copy(k, target, number(source)).wait_recv())

    for j in range(NF):
        total = arrived[j * R]
        for r in range(1, R):
            total = total + arrived[j * R + r]
        tidy[j : j + 1, :] = total[0:1]
        tidy[NF + j : NF + j + 1, :] = total[1:2]
    part = rep if REP == PB else lax.rem(me, PB)
    value = tidy[:, :TL]
    for h in range(1, PB):
        value = jnp.where(part == h, tidy[:, h * TL : (h + 1) * TL], value)
    prim_v[...] = spectrum.astype(F32)[: 2 * NF] - value

    each_peer(lambda k, target, source: pick_copy(k, target, me).wait_send())
    for c in range(CHUNKS):
        for n in range(R - 1):
            panel_copy(n, c, reader).wait_send()
        out_copy(c).wait()


def local(traces, data, trace_shot, trace_recv, aper_panel, aper_order, aper_count):
    NF = lax.axis_size("freq") * data.shape[0]
    PAN, REP = lax.axis_size("pan"), lax.axis_size("rep")
    R = PAN * REP
    N = NF * R
    SW, NS = data.shape[2], data.shape[3]
    TL, NT = traces.shape
    total = trace_shot.shape[0]
    GROUP = min(total, 1024)
    W = NS // CHUNKS
    RK = R * KB
    table = jnp.asarray(spectral_table(NT, NF, FBIN0, FSTEP))
    sizes = (NF, PAN, REP, SW, NS, TL, GROUP)
    vmem = pl.BlockSpec(memory_space=pltpu.VMEM)
    hbm = pl.BlockSpec(memory_space=pltpu.HBM)
    anywhere = pl.BlockSpec(memory_space=pl.ANY)
    multiples, primaries = pl.pallas_call(
        functools.partial(kernel, sizes),
        out_shape=(
            jax.ShapeDtypeStruct((1, 2, SW, NS), BF),
            jax.ShapeDtypeStruct((2 * NF, TL), F32),
        ),
        in_specs=[hbm] * 8,
        out_specs=(anywhere, vmem),
        scratch_shapes=[
            pltpu.SMEM((R, R), jnp.int32),
            pltpu.SMEM((R, R), jnp.int32),
            pltpu.SMEM((R,), jnp.int32),
            pltpu.VMEM((total // LANES, LANES), jnp.int32),
            pltpu.VMEM((total // LANES, LANES), jnp.int32),
            pltpu.VMEM((2, SW // KB, KB, NS), BF),
            pltpu.VMEM((TL, NT), BF),
            pltpu.VMEM(table.shape, BF),
            pltpu.VMEM((R - 1, CHUNKS, 2, KB, W), BF),
            pltpu.VMEM((CHUNKS, 2, R, KB, W), BF),
            pltpu.VMEM((NS, RK), BF),
            pltpu.VMEM((SW, 2 * RK), BF),
            pltpu.VMEM((SW, 2 * RK), BF),
            pltpu.VMEM((2 * RK, SW), BF),
            pltpu.VMEM((NS, GROUP), BF),
            pltpu.VMEM((2 * RK, GROUP), F32),
            pltpu.VMEM((8, GROUP), F32),
            pltpu.VMEM((total // LANES, 8, LANES), F32),
            pltpu.VMEM((N, 8, LANES), F32),
            pltpu.VMEM((2 * NF, LANES), F32),
            pltpu.VMEM((CHUNKS, 2, SW, W), BF),
            pltpu.SemaphoreType.DMA((8,)),
            pltpu.SemaphoreType.DMA((R - 1, CHUNKS)),
            pltpu.SemaphoreType.DMA((R - 1, CHUNKS)),
            pltpu.SemaphoreType.DMA((N,)),
            pltpu.SemaphoreType.DMA((N,)),
            pltpu.SemaphoreType.DMA((CHUNKS,)),
        ],
        compiler_params=pltpu.CompilerParams(
            collective_id=0, has_side_effects=True, vmem_limit_bytes=48 * 1024 * 1024
        ),
    )(
        *(
            pltpu.with_memory_space_constraint(operand, pltpu.HBM)
            for operand in (
                data.reshape(1, 2, SW // KB, KB, NS),
                traces,
                table,
                aper_panel,
                aper_order,
                aper_count,
                trace_shot.reshape(-1, LANES),
                trace_recv.reshape(-1, LANES),
            )
        )
    )
    return multiples, jnp.transpose(primaries.reshape(2, NF, TL), (2, 0, 1))


def solution(mesh):
    in_specs = (
        P(("parts", "freq", "pan", "rep"), None),
        P(("parts", "freq"), None, ("pan", "rep"), None),
        P("parts"),
        P("parts"),
        P("parts", None),
        P("parts", None),
        P("parts"),
    )
    out_specs = (
        P(("parts", "freq"), None, ("pan", "rep"), None),
        P(("parts", "freq", "pan", "rep"), None, None),
    )
    return jax.shard_map(local, mesh=mesh, in_specs=in_specs, out_specs=out_specs, check_vma=False)
```

```python
import functools
import math

import jax
import jax.numpy as jnp
import numpy as np
from jax import lax
from jax.experimental import pallas as pl
from jax.experimental.pallas import tpu as pltpu
from jax.sharding import PartitionSpec as P

KB = 32
FBIN0 = 64
FSTEP = 3
LANES = 128
CHUNKS = 4
BLOCK = 2 * LANES
MESH = pl.DeviceIdType.MESH
BF = jnp.bfloat16
F32 = jnp.float32


def spectral_table(samples, count, first, stride):
    times = np.arange(samples, dtype=np.int32)
    bins = first + stride * np.arange(count, dtype=np.int32)
    phase = bins[:, None] * times[None, :] % samples
    angle = phase.astype(np.float32) * np.float32(2.0 * math.pi / samples)
    factor = np.float32(1.0 / math.sqrt(samples))
    rows = np.concatenate([np.cos(angle) * factor, -np.sin(angle) * factor], axis=0)
    padded = np.zeros((-(-rows.shape[0] // 16) * 16, samples), np.float32)
    padded[: rows.shape[0]] = rows
    return padded.astype(jnp.bfloat16)


def kernel(
    sizes,
    data_hbm, traces_hbm, table_hbm, panel_hbm, order_hbm, count_hbm, shot_hbm, recv_hbm,
    out_hbm, prim_v,
    panel_s, order_s, count_s, shot_v, recv_v, data_v, traces_v, table_v, send, panels, sel, left_a, left_b, left_t, hot, lsel, acc, picks,
    arrived, tidy, stage,
    load_sem, send_sem, recv_sem, pick_send, pick_recv, out_sem,
):
    NF, PAN, REP, SW, NS, TL, GROUP = sizes
    R = PAN * REP
    N = NF * R
    RK = R * KB
    W = NS // CHUNKS
    PB = LANES // TL
    freq, pan, rep = lax.axis_index("freq"), lax.axis_index("pan"), lax.axis_index("rep")
    reader = pan * REP + rep
    me = freq * R + reader

    def turn(at, step, size):
        return at if isinstance(step, int) and step == 0 else lax.rem(at + step, size)

    pans = [turn(pan, k, PAN) for k in range(PAN)]
    reps = [turn(rep, k, REP) for k in range(REP)]
    back_pans = [turn(pan, PAN - k, PAN) if k else pan for k in range(PAN)]
    back_reps = [turn(rep, REP - k, REP) if k else rep for k in range(REP)]

    def each_peer(act):
        def band(k):
            there = turn(freq, k, NF)
            back = freq if isinstance(k, int) and k == 0 else lax.rem(freq + NF - k, NF)
            for dp in range(PAN):
                for dr in range(REP):
                    if isinstance(k, int) and (k, dp, dr) == (0, 0, 0):
                        continue
                    act(
                        k * R + dp * REP + dr,
                        (there, pans[dp], reps[dr]),
                        (back, back_pans[dp], back_reps[dr]),
                    )

        band(0)
        if N <= 32:
            for k in range(1, NF):
                band(k)
        else:
            pl.loop(1, NF)(band)

    def place(spot):
        return {"freq": spot[0], "pan": spot[1], "rep": spot[2]}

    def number(spot):
        return spot[0] * R + spot[1] * REP + spot[2]

    def lane_block(spot):
        return spot[0] * PAN + spot[1] if REP == PB else lax.div(number(spot), PB)

    loads = [
        pltpu.make_async_copy(panel_hbm, panel_s, load_sem.at[0]),
        pltpu.make_async_copy(data_hbm.at[0], data_v, load_sem.at[1]),
        pltpu.make_async_copy(order_hbm, order_s, load_sem.at[2]),
        pltpu.make_async_copy(count_hbm, count_s, load_sem.at[3]),
        pltpu.make_async_copy(shot_hbm, shot_v, load_sem.at[4]),
        pltpu.make_async_copy(recv_hbm, recv_v, load_sem.at[5]),
        pltpu.make_async_copy(traces_hbm, traces_v, load_sem.at[6]),
        pltpu.make_async_copy(table_hbm, table_v, load_sem.at[7]),
    ]
    for copy in loads:
        copy.start()

    barrier = pltpu.get_barrier_semaphore()

    each_peer(
        lambda k, target, source: pl.semaphore_signal(
            barrier, inc=1, device_id=place(target), device_id_type=MESH
        )
    )

    loads[0].wait()
    loads[1].wait()
    offsets = [(dp, dr) for dp in range(PAN) for dr in range(REP) if (dp, dr) != (0, 0)]
    offsets = [o for o in offsets if o[0]] + [o for o in offsets if not o[0]]

    for n, (dp, dr) in enumerate(offsets):
        p = panel_s[pans[dp] * REP + reps[dr], reader]
        for c in range(CHUNKS):
            send[n, c] = data_v[:, p, :, c * W : (c + 1) * W]
    pl.semaphore_wait(barrier, N - 1)

    def panel_copy(n, c, slot):
        dp, dr = offsets[n]
        return pltpu.make_async_remote_copy(
            src_ref=send.at[n, c],
            dst_ref=panels.at[c, :, slot],
            send_sem=send_sem.at[n, c],
            recv_sem=recv_sem.at[n, c],
            device_id={"pan": pans[dp], "rep": reps[dr]},
            device_id_type=MESH,
        )

    for c in range(CHUNKS):
        for n in range(R - 1):
            panel_copy(n, c, reader).start()
    p = panel_s[reader, reader]
    for c in range(CHUNKS):
        panels[c, :, reader] = data_v[:, p, :, c * W : (c + 1) * W]

    loads[2].wait()
    loads[3].wait()
    lane = lax.broadcasted_iota(jnp.int32, (1, RK), 1)
    column = jnp.full((1, RK), -1, jnp.int32)
    for q in range(R):
        hit = jnp.int32(0)
        for m in range(R):
            named = (order_s[reader, m] == q).astype(jnp.int32)
            hit = hit + named * (count_s[reader] > m).astype(jnp.int32)
        base = hit * (q * SW + panel_s[reader, q] * KB - q * KB + 2 * NS) - 2 * NS
        column = jnp.where((lane >= q * KB) & (lane < (q + 1) * KB), lane + base, column)

    @pl.loop(0, NS // 256)
    def _(b):
        at = pl.multiple_of(b * 256, 256)
        rows = lax.broadcasted_iota(jnp.int32, (256, RK), 0) + at
        sel[pl.ds(at, 256), :] = jnp.where(rows == column, 1.0, 0.0).astype(BF)

    BAND = min(SW, 512)

    @pl.loop(0, SW // BAND)
    def _(b):
        rows = pl.ds(pl.multiple_of(b * BAND, BAND), BAND)
        strips = pl.ds(b * (BAND // KB), BAND // KB)
        real = jnp.dot(
            data_v[0, strips].reshape(BAND, NS), sel[...], preferred_element_type=F32
        )
        imag = jnp.dot(
            data_v[1, strips].reshape(BAND, NS), sel[...], preferred_element_type=F32
        )
        left_a[rows, :RK] = real.astype(BF)
        left_a[rows, RK:] = (-imag).astype(BF)
        left_b[rows, :RK] = imag.astype(BF)
        left_b[rows, RK:] = real.astype(BF)

    left_t[...] = left_a[...].T

    for copy in loads[4:]:
        copy.wait()
    spectrum = lax.dot_general(
        table_v[...], traces_v[...], (((1,), (1,)), ((), ())), preferred_element_type=F32
    ).astype(BF)

    blocks = GROUP // BLOCK

    def prepare(g):
        @pl.loop(0, blocks)
        def _(b):
            lanes = pl.ds(pl.multiple_of(b * BLOCK, BLOCK), BLOCK)
            row = (g * blocks + b) * 2
            recv = jnp.concatenate([recv_v[pl.ds(row, 1), :], recv_v[pl.ds(row + 1, 1), :]], axis=1)
            shot = jnp.concatenate([shot_v[pl.ds(row, 1), :], shot_v[pl.ds(row + 1, 1), :]], axis=1)
            for c in range(NS // 256):
                rows = lax.broadcasted_iota(jnp.int32, (256, BLOCK), 0) + c * 256
                hot[c * 256 : (c + 1) * 256, lanes] = jnp.where(rows == recv, 1.0, 0.0).astype(BF)
            mine = lax.broadcasted_iota(jnp.int32, (SW, BLOCK), 0) + reader * SW
            mine = jnp.where(mine == shot, 1.0, 0.0).astype(BF)
            lsel[:, lanes] = jnp.dot(left_t[...], mine, preferred_element_type=F32)

    def pick(c):
        @pl.loop(0, blocks)
        def _(b):
            lanes = pl.ds(pl.multiple_of(b * BLOCK, BLOCK), BLOCK)
            got = jnp.dot(
                panels[c].reshape(2 * RK, W),
                hot[c * W : (c + 1) * W, lanes],
                preferred_element_type=F32,
            )
            lefts = lsel[:, lanes]
            real = jnp.sum(lefts * got, axis=0, keepdims=True)
            imag = jnp.sum(lefts[:RK] * got[RK:] - lefts[RK:] * got[:RK], axis=0, keepdims=True)
            if c == 0:
                acc[0:1, lanes] = real
                acc[1:2, lanes] = imag
            else:
                acc[0:1, lanes] += real
                acc[1:2, lanes] += imag

    def keep(g):
        for i in range(GROUP // LANES):
            value = acc[0:2, i * LANES : (i + 1) * LANES].astype(BF).astype(F32)
            picks[g * (GROUP // LANES) + i, 0:2, :] = value

    def multiply(c):
        @pl.loop(0, SW // 128)
        def _(b):
            rows = pl.ds(pl.multiple_of(b * 128, 128), 128)
            right = panels[c].reshape(2 * RK, W)
            stage[c, 0, rows, :] = jnp.dot(
                left_a[rows, :], right, preferred_element_type=F32
            ).astype(BF)
            stage[c, 1, rows, :] = jnp.dot(
                left_b[rows, :], right, preferred_element_type=F32
            ).astype(BF)

        out_copy(c).start()

    def out_copy(c):
        return pltpu.make_async_copy(
            stage.at[c], out_hbm.at[0, :, :, pl.ds(c * W, W)], out_sem.at[c]
        )

    picks[...] = jnp.zeros_like(picks)
    prepare(0)
    for c in range(CHUNKS):
        for n, (dp, dr) in enumerate(offsets):
            sender = back_pans[dp] * REP + back_reps[dr]
            panel_copy(n, c, sender).wait_recv()
        pick(c)
        if c < CHUNKS - 1:
            multiply(c)
    keep(0)

    @pl.loop(1, (NF * R * TL) // GROUP)
    def _(g):
        prepare(g)
        for c in range(CHUNKS):
            pick(c)
        keep(g)

    def pick_copy(k, target, slot):
        return pltpu.make_async_remote_copy(
            src_ref=picks.at[lane_block(target)],
            dst_ref=arrived.at[slot],
            send_sem=pick_send.at[k],
            recv_sem=pick_recv.at[k],
            device_id=place(target),
            device_id_type=MESH,
        )

    each_peer(lambda k, target, source: pick_copy(k, target, me).start())
    arrived[me] = picks[lane_block((freq, pan, rep))]
    multiply(CHUNKS - 1)
    each_peer(lambda k, target, source: pick_copy(k, target, number(source)).wait_recv())

    for j in range(NF):
        total = arrived[j * R]
        for r in range(1, R):
            total = total + arrived[j * R + r]
        tidy[j : j + 1, :] = total[0:1]
        tidy[NF + j : NF + j + 1, :] = total[1:2]
    part = rep if REP == PB else lax.rem(me, PB)
    value = tidy[:, :TL]
    for h in range(1, PB):
        value = jnp.where(part == h, tidy[:, h * TL : (h + 1) * TL], value)
    prim_v[...] = spectrum.astype(F32)[: 2 * NF] - value

    each_peer(lambda k, target, source: pick_copy(k, target, me).wait_send())
    for c in range(CHUNKS):
        for n in range(R - 1):
            panel_copy(n, c, reader).wait_send()
        out_copy(c).wait()


def local(traces, data, trace_shot, trace_recv, aper_panel, aper_order, aper_count):
    NF = lax.axis_size("freq") * data.shape[0]
    PAN, REP = lax.axis_size("pan"), lax.axis_size("rep")
    R = PAN * REP
    N = NF * R
    SW, NS = data.shape[2], data.shape[3]
    TL, NT = traces.shape
    total = trace_shot.shape[0]
    GROUP = min(total, 1024)
    W = NS // CHUNKS
    RK = R * KB
    table = jnp.asarray(spectral_table(NT, NF, FBIN0, FSTEP))
    sizes = (NF, PAN, REP, SW, NS, TL, GROUP)
    vmem = pl.BlockSpec(memory_space=pltpu.VMEM)
    hbm = pl.BlockSpec(memory_space=pltpu.HBM)
    anywhere = pl.BlockSpec(memory_space=pl.ANY)
    multiples, primaries = pl.pallas_call(
        functools.partial(kernel, sizes),
        out_shape=(
            jax.ShapeDtypeStruct((1, 2, SW, NS), BF),
            jax.ShapeDtypeStruct((2 * NF, TL), F32),
        ),
        in_specs=[hbm] * 8,
        out_specs=(anywhere, vmem),
        scratch_shapes=[
            pltpu.SMEM((R, R), jnp.int32),
            pltpu.SMEM((R, R), jnp.int32),
            pltpu.SMEM((R,), jnp.int32),
            pltpu.VMEM((total // LANES, LANES), jnp.int32),
            pltpu.VMEM((total // LANES, LANES), jnp.int32),
            pltpu.VMEM((2, SW // KB, KB, NS), BF),
            pltpu.VMEM((TL, NT), BF),
            pltpu.VMEM(table.shape, BF),
            pltpu.VMEM((R - 1, CHUNKS, 2, KB, W), BF),
            pltpu.VMEM((CHUNKS, 2, R, KB, W), BF),
            pltpu.VMEM((NS, RK), BF),
            pltpu.VMEM((SW, 2 * RK), BF),
            pltpu.VMEM((SW, 2 * RK), BF),
            pltpu.VMEM((2 * RK, SW), BF),
            pltpu.VMEM((NS, GROUP), BF),
            pltpu.VMEM((2 * RK, GROUP), F32),
            pltpu.VMEM((8, GROUP), F32),
            pltpu.VMEM((total // LANES, 8, LANES), F32),
            pltpu.VMEM((N, 8, LANES), F32),
            pltpu.VMEM((2 * NF, LANES), F32),
            pltpu.VMEM((CHUNKS, 2, SW, W), BF),
            pltpu.SemaphoreType.DMA((8,)),
            pltpu.SemaphoreType.DMA((R - 1, CHUNKS)),
            pltpu.SemaphoreType.DMA((R - 1, CHUNKS)),
            pltpu.SemaphoreType.DMA((N,)),
            pltpu.SemaphoreType.DMA((N,)),
            pltpu.SemaphoreType.DMA((CHUNKS,)),
        ],
        compiler_params=pltpu.CompilerParams(
            collective_id=0, has_side_effects=True, vmem_limit_bytes=48 * 1024 * 1024
        ),
    )(
        *(
            pltpu.with_memory_space_constraint(operand, pltpu.HBM)
            for operand in (
                data.reshape(1, 2, SW // KB, KB, NS),
                traces,
                table,
                aper_panel,
                aper_order,
                aper_count,
                trace_shot.reshape(-1, LANES),
                trace_recv.reshape(-1, LANES),
            )
        )
    )
    return multiples, jnp.transpose(primaries.reshape(2, NF, TL), (2, 0, 1))


def solution(mesh):
    in_specs = (
        P(("parts", "freq", "pan", "rep"), None),
        P(("parts", "freq"), None, ("pan", "rep"), None),
        P("parts"),
        P("parts"),
        P("parts", None),
        P("parts", None),
        P("parts"),
    )
    out_specs = (
        P(("parts", "freq"), None, ("pan", "rep"), None),
        P(("parts", "freq", "pan", "rep"), None, None),
    )
    return jax.shard_map(local, mesh=mesh, in_specs=in_specs, out_specs=out_specs, check_vma=False)
```
